128 devices in a mesh: row: 8 (over x, core), col: 16 (over y, z).
Axes of the slice: x: 4, y: 4, z: 4, core: 2. Of those that a mesh axis runs over, the one named last changes fastest.
Arguments:
- inputs: bfloat16 [1024, 6144], P('row', 'col'), may hold values from -6 to 6
- upstream: bfloat16 [1024, 6144], P('row', 'col'), may hold values from -6 to 6
- preact: bfloat16 [1024, 24576], P('col', 'row'), may hold values from -6 to 6
- bias_in: float32 [24576], P('row'), may hold values from -3 to 3
- w_in: bfloat16 [6144, 24576], P('col', 'row'), may hold values from -0.078125 to 0.078125
- w_out: bfloat16 [24576, 6144], P('row', 'col'), may hold values from -0.0390625 to 0.0390625
- lengths: int32 [8], replicated, may hold values from 1 to 256, 1024 in all
Outputs:
- grad_inputs: bfloat16 [1024, 6144], P('row', 'col')
- grad_w_in: bfloat16 [6144, 24576], P('col', 'row')
- grad_w_out: bfloat16 [24576, 6144], P('row', 'col')
The draws below stay inside these ranges and needn't reach their ends.
All inputs are finite; a program needn't handle non-finite values.
Results may differ from the reference program's by a relative error of at most 0.0058.
Values may be sent and summed in bfloat16 or wider, within the bound.
No kernel may reach another device: no remote copies, remote signals or barrier semaphores. Data moves between devices by JAX's collectives and lax.ppermute only.
A program may use at most 128 MiB of HBM per device.

```python
import math
import jax
import jax.numpy as jnp
import numpy as np
from jax import lax

D = 6144
F = 24576
IMAGES = 8
ROWS = 1024
MOST = 256


def level_of(own_key, dims, pieces, low, high):
    gain, own = 1.0, jax.random.fold_in(own_key, 6)
    for dim, shards_of in pieces:
        heights = jnp.exp(jax.random.uniform(jax.random.fold_in(own, dim), (shards_of,), jnp.float32, low / len(pieces), high / len(pieces)))
        gain = gain * jnp.repeat(heights, dims[dim] // shards_of).reshape([-1 if axis == dim else 1 for axis in range(len(dims))])
    return gain


def profile(count, total, most, skew):
    loads = [(1 << 20) // math.isqrt(rank ** skew) + 1 for rank in range(2, count + 1)]
    rest, counts = total - most - (count - 1), [1] * (count - 1)
    while rest > 0:
        candidates = [i for i in range(count - 1) if counts[i] < most]
        pool, left = sum([loads[i] for i in candidates]), rest
        for i in candidates:
            extra = min(most - counts[i], max(1, left * loads[i] // pool), rest)
            counts[i] = counts[i] + extra
            rest = rest - extra
    return np.array([most] + counts)


def ragged(own_key, amount, total, reach, skew):
    if amount == 2:
        one = jax.random.randint(own_key, (), max(1, total - reach), min(reach, total - 1) + 1)
        return jnp.stack([one, total - one])
    tallies = jnp.asarray(profile(amount, total, reach, skew), jnp.int32)
    pairs = (amount - 1) // 2
    giver, sink = tallies[1:1 + 2 * pairs:2], tallies[2:2 + 2 * pairs:2]
    room = jnp.minimum(giver - 1, reach - sink)
    passed = jax.random.randint(jax.random.fold_in(own_key, 1), (pairs,), 0, 1 << 20) % (room + 1)
    tallies = tallies.at[1:1 + 2 * pairs:2].set(giver - passed).at[2:2 + 2 * pairs:2].set(sink + passed)
    return tallies[jax.random.permutation(jax.random.fold_in(own_key, 2), amount)]


def normal_values(key, shape, width, most, split=(), kind=jnp.bfloat16):
    level = level_of(key, shape, split, -0.22, 0.18) if split else 1.0
    values = jax.random.normal(key, shape, jnp.float32) * width * level
    return jnp.minimum(jnp.maximum(values, -most), most).astype(kind)


def setup_inputs(seed: int = 0) -> dict:
    seeds = jax.random.split(jax.random.key(seed), 8)
    inputs = normal_values(seeds[0], (ROWS, D), 1.0, 6.0, ((0, 8), (1, 16)))
    upstream = normal_values(seeds[1], (ROWS, D), 1.0, 6.0, ((0, 8), (1, 16)))
    preact = normal_values(seeds[2], (ROWS, F), 1.0, 6.0, ((0, 16), (1, 8)))
    bias_in = normal_values(seeds[3], (F,), 0.5, 3.0, ((0, 8),), jnp.float32)
    w_in = normal_values(seeds[4], (D, F), D ** -0.5, 0.078125, ((0, 16), (1, 8)))
    w_out = normal_values(seeds[5], (F, D), F ** -0.5, 0.0390625, ((0, 8), (1, 16)))
    lengths = ragged(seeds[6], IMAGES, ROWS, MOST, 2).astype(jnp.int32)
    return dict(inputs=inputs, upstream=upstream, preact=preact, bias_in=bias_in, w_in=w_in, w_out=w_out, lengths=lengths)


def token_weights(lengths, first_row, count, rows_total):
    ends = jnp.cumsum(lengths)
    starts = ends - lengths
    position = first_row + jnp.arange(count, dtype=jnp.int32)
    member = (position[:, None] >= starts[None, :]) & (position[:, None] < ends[None, :])
    size = lax.optimization_barrier(jnp.sum(jnp.where(member, lengths[None, :], 0), axis=1)).astype(jnp.float32)
    return jnp.sqrt(rows_total / IMAGES / size)

def gelu_parts(pre):
    normal_cdf = 0.5 * (1.0 + lax.erf(pre * 0.7071067811865476))
    density = jnp.exp(-0.5 * pre * pre) * 0.3989422804014327
    return (pre * normal_cdf, normal_cdf + pre * density)

def reference(inputs, upstream, preact, bias_in, w_in, w_out, lengths):
    weight = token_weights(lengths, 0, ROWS, ROWS)
    scaled = (upstream.astype(jnp.float32) * weight[:, None]).astype(jnp.bfloat16)
    pre = preact.astype(jnp.float32) + bias_in[None, :]
    value, slope = gelu_parts(pre)
    act = value.astype(jnp.bfloat16)
    back = lax.dot_general(scaled, w_out, (((1,), (1,)), ((), ())), preferred_element_type=jnp.float32)
    grad_pre = (back * slope).astype(jnp.bfloat16)
    factor = ROWS ** (-0.5)
    grad_w_out = (lax.dot_general(act, scaled, (((0,), (0,)), ((), ())), preferred_element_type=jnp.float32) * factor).astype(jnp.bfloat16)
    grad_w_in = (lax.dot_general(inputs, grad_pre, (((0,), (0,)), ((), ())), preferred_element_type=jnp.float32) * factor).astype(jnp.bfloat16)
    grad_inputs = lax.dot_general(grad_pre, w_in, (((1,), (1,)), ((), ())), preferred_element_type=jnp.float32).astype(jnp.bfloat16)
    return (grad_inputs, grad_w_in, grad_w_out)
```

```python
import functools

import jax
import jax.numpy as jnp
from jax import lax
from jax.experimental import pallas as pl
from jax.experimental.pallas import tpu as pltpu
from jax.sharding import PartitionSpec as P

IMAGES = 8
SIDE = 4
BLOCK = 64
WIDE = 512
SPLIT = 1536
F32, BF16 = jnp.float32, jnp.bfloat16
NT = (((1,), (1,)), ((), ()))
NN = (((1,), (0,)), ((), ()))


def dot(left, right, dims):
    return lax.dot_general(left, right, dims, preferred_element_type=F32)


def gelu_parts(pre):
    normal_cdf = 0.5 * (1.0 + lax.erf(pre * 0.7071067811865476))
    density = jnp.exp(-0.5 * pre * pre) * 0.3989422804014327
    return (pre * normal_cdf, normal_cdf + pre * density)


def move_y(a, by):
    pairs = [(4 * y + z, 4 * ((y + by) % SIDE) + z) for y in range(SIDE) for z in range(SIDE)]
    return lax.ppermute(a, "col", pairs)


def move_z(a, by):
    pairs = [(4 * y + z, 4 * y + (z + by) % SIDE) for y in range(SIDE) for z in range(SIDE)]
    return lax.ppermute(a, "col", pairs)


def move_x(a, by):
    pairs = [(2 * x + c, 2 * ((x + by) % SIDE) + c) for x in range(SIDE) for c in range(2)]
    return lax.ppermute(a, "row", pairs)


def swap_core(a):
    return lax.ppermute(a, "row", [(2 * x + c, 2 * x + 1 - c) for x in range(SIDE) for c in range(2)])


def call(kernel, outs, operands, name, grid=(), in_specs=None, out_specs=None, flops=0, scratch=(), alias=None):
    moved = sum(o.size * o.dtype.itemsize for o in operands) + sum(o.size * o.dtype.itemsize for o in outs)
    return pl.pallas_call(
        kernel,
        out_shape=outs,
        grid=grid,
        in_specs=in_specs,
        out_specs=out_specs,
        scratch_shapes=scratch,
        input_output_aliases=alias or {},
        name=name,
        cost_estimate=pl.CostEstimate(flops=flops, bytes_accessed=moved, transcendentals=0),
        compiler_params=pltpu.CompilerParams(vmem_limit_bytes=48 * 2**20),
    )(*operands)


SMEM = pl.BlockSpec(memory_space=pltpu.SMEM)
VMEM = pl.BlockSpec(memory_space=pltpu.VMEM)


def shape(dims, kind):
    return jax.ShapeDtypeStruct(dims, kind)


def whole(dims):
    return pl.BlockSpec(dims, lambda i: (0, 0))


def gathered_block(place, mine, other, y, z):
    start = pl.multiple_of(((y - place[2]) & 3) * 128 + (z % 2) * BLOCK, BLOCK)
    rows = pl.ds(start, BLOCK)
    return jnp.where(place[3] == z // 2, mine[rows, :], other[rows, :])


def relative(place, y, z):
    return (y - place[0]) & 3, (z - place[1]) & 3


def rows_of(major, minor):
    return pl.ds(pl.multiple_of((major * SIDE + minor) * BLOCK, BLOCK), BLOCK)


def scaled_kernel(place, lengths, mine, other, by_z, by_y, flipped, plain):
    for y in range(SIDE):
        for z in range(SIDE):
            block = gathered_block(place, mine, other, y, z)
            position = (y * SIDE + z) * BLOCK + lax.broadcasted_iota(jnp.int32, block.shape, 0)
            size = jnp.zeros(block.shape, jnp.int32)
            start = 0
            for k in range(IMAGES):
                end = start + lengths[k]
                size = jnp.where((position >= start) & (position < end), lengths[k], size)
                start = end
            weight = jnp.sqrt(128.0 / size.astype(F32))
            block = (block.astype(F32) * weight).astype(BF16)
            dy, dz = relative(place, y, z)
            by_z[rows_of(dz, dy), :] = block
            by_y[rows_of(dy, dz), :] = block
            plain[pl.ds((y * SIDE + z) * BLOCK, BLOCK), :] = block
    flipped[...] = plain[...].T


def inputs_kernel(place, mine, other, by_z, by_y, first, second):
    for y in range(SIDE):
        for z in range(SIDE):
            block = gathered_block(place, mine, other, y, z)
            dy, dz = relative(place, y, z)
            first[rows_of(dz, dy), :] = block
            second[rows_of(dy, dz), :] = block
    by_z[...] = first[...].T
    by_y[...] = second[...].T


def first_kernel(scaled, w, plus, minus):
    both = dot(scaled[384:896, :], w[...], NT).astype(BF16)
    plus[...] = both[:256]
    minus[...] = both[256:]


def second_kernel(scaled, w, from_low, from_high, plus, minus):
    plus[...] = (dot(scaled[256:384, :], w[...], NT) + from_low[...].astype(F32)).astype(BF16)
    minus[...] = (dot(scaled[896:1024, :], w[...], NT) + from_high[...].astype(F32)).astype(BF16)


def third_kernel(scaled, w, low_own, high_own, low_sum, high_sum, own, one, two, three):
    total = dot(scaled[0:256, :], w[...], NT)
    upper = total[:128] + high_own[...].astype(F32) + low_sum[...].astype(F32)
    lower = total[128:] + low_own[...].astype(F32) + high_sum[...].astype(F32)
    own[...] = upper[:64]
    one[...] = upper[64:].astype(BF16)
    two[...] = lower[:64].astype(BF16)
    three[...] = lower[64:].astype(BF16)


def slope_kernel(own, one, two, three, slope, grad):
    back = own[...] + one[...].astype(F32) + two[...].astype(F32) + three[...].astype(F32)
    grad[...] = (back * slope[...]).astype(BF16)


def reduce_group(scaled, w_out, slope, first, width, major, minor):
    steps, skip = width // WIDE, first // WIDE
    depth = scaled.shape[1]
    s_spec = whole(scaled.shape)
    w_spec = pl.BlockSpec((WIDE, depth), lambda i: (i + skip, 0))

    def part(rows, at=0):
        return pl.BlockSpec((rows, WIDE), lambda i: (at, i))

    plus, minus = call(
        first_kernel,
        [shape((256, width), BF16)] * 2,
        (scaled, w_out),
        "back_first",
        (steps,),
        [s_spec, w_spec],
        [part(256)] * 2,
        2 * 512 * depth * width,
    )
    low, high = major(plus, 1), major(minus, -1)
    plus, minus = call(
        second_kernel,
        [shape((128, width), BF16)] * 2,
        (scaled, w_out, low, high),
        "back_second",
        (steps,),
        [s_spec, w_spec, part(128, 1), part(128, 0)],
        [part(128)] * 2,
        2 * 256 * depth * width,
    )
    low_sum, high_sum = major(plus, 1), major(minus, -1)
    own, one, two, three = call(
        third_kernel,
        [shape((64, width), F32)] + [shape((64, width), BF16)] * 3,
        (scaled, w_out, low, high, low_sum, high_sum),
        "back_third",
        (steps,),
        [s_spec, w_spec, part(128, 0), part(128, 1), part(128), part(128)],
        [part(64)] * 4,
        2 * 256 * depth * width,
    )
    one, two, three = minor(one, 1), minor(two, 2), minor(three, 3)
    return call(
        slope_kernel,
        [shape((64, width), BF16)],
        (own, one, two, three, slope),
        "grad_pre",
        (steps,),
        [part(64)] * 4 + [pl.BlockSpec((64, WIDE), lambda i: (0, i + skip))],
        [part(64)],
    )[0]


def gather_group(grad, major, minor):
    near = jnp.concatenate([grad, minor(grad, -1), minor(grad, -2), minor(grad, -3)], axis=0)
    low, high = major(near, 1), major(near, -1)
    return near, high, major(low[:128], 1), major(high[128:], -1), low


def all_rows(pieces):
    return jnp.concatenate([piece[...] for piece in pieces], axis=0)


def piece_specs():
    return [pl.BlockSpec((rows, WIDE), lambda i: (0, i)) for rows in (256, 256, 128, 128, 256)]


def grad_inputs_kernel(one, two, three, four, five, w, total):
    part = dot(all_rows((one, two, three, four, five)), w[...], NT)

    @pl.when(pl.program_id(0) == 0)
    def _():
        total[...] = part

    @pl.when(pl.program_id(0) > 0)
    def _():
        total[...] += part


def grad_inputs_group(pieces, w_in, first):
    width, depth = pieces[0].shape[1], w_in.shape[0]
    skip = first // WIDE
    return call(
        grad_inputs_kernel,
        [shape((1024, depth), F32)],
        (*pieces, w_in),
        "grad_inputs",
        (width // WIDE,),
        piece_specs() + [pl.BlockSpec((depth, WIDE), lambda i: (0, i + skip))],
        [whole((1024, depth))],
        2 * 1024 * depth * width,
    )[0]


def join_kernel(place, by_z, by_y, send, keep):
    for far in range(SIDE):
        for z in range(2):
            for out, core in ((keep, place[3]), (send, 1 - place[3])):
                dy, dz = relative(place, place[2] + far, 2 * core + z)
                block = by_z[rows_of(dz, dy), :] + by_y[rows_of(dy, dz), :]
                out[pl.ds(far * 128 + z * BLOCK, BLOCK), :] = block.astype(out.dtype)


def grad_w_in_kernel(factor, flipped, one, two, three, four, five, *rest):
    rest[-1][...] = (dot(flipped[...], all_rows((one, two, three, four, five)), NN) * factor).astype(BF16)


def grad_w_in_group(flipped, pieces, first, factor, total, so_far):
    width, depth = pieces[0].shape[1], flipped.shape[0]
    skip = first // WIDE
    operands = (flipped, *pieces) + (() if so_far is None else (so_far,))
    return call(
        functools.partial(grad_w_in_kernel, factor),
        [shape((depth, total), BF16)],
        operands,
        "grad_w_in",
        (width // WIDE,),
        [whole(flipped.shape)] + piece_specs() + [pl.BlockSpec(memory_space=pl.ANY)] * (len(operands) - 6),
        [pl.BlockSpec((depth, WIDE), lambda i: (0, i + skip))],
        2 * 1024 * depth * width,
        alias=None if so_far is None else {6: 0},
    )[0]


def grad_w_out_kernel(factor, flipped, act, out):
    out[...] = (dot(flipped[...], act[...], NN) * factor).T.astype(BF16)


def grad_w_out_all(flipped, act, factor):
    depth, width = flipped.shape[0], act.shape[1]
    return call(
        functools.partial(grad_w_out_kernel, factor),
        [shape((width, depth), BF16)],
        (flipped, act),
        "grad_w_out",
        (width // WIDE,),
        [whole(flipped.shape), pl.BlockSpec((1024, WIDE), lambda i: (0, i))],
        [pl.BlockSpec((WIDE, depth), lambda i: (i, 0))],
        2 * 1024 * depth * width,
    )[0]


def row_gather(a):
    mine = jnp.concatenate([a, move_x(a, -1), move_x(a, -2), move_x(a, -3)], axis=0)
    return mine, swap_core(mine)


def shards(inputs, upstream, preact, bias_in, w_in, w_out, lengths):
    col, row = lax.axis_index("col"), lax.axis_index("row")
    place = jnp.stack([col // SIDE, col % SIDE, row // 2, row % 2]).astype(jnp.int32)
    depth, hidden = w_in.shape
    factor = 1024 ** (-0.5)

    up_mine, up_other = row_gather(upstream)
    scaled_z, scaled_y, scaled_flipped = call(
        scaled_kernel,
        [shape((1024, depth), BF16)] * 2 + [shape((depth, 1024), BF16)],
        (place, lengths, up_mine, up_other),
        "scaled",
        in_specs=[SMEM, SMEM, VMEM, VMEM],
        out_specs=[VMEM] * 3,
        scratch=[pltpu.VMEM((1024, depth), BF16)],
    )
    pre = preact.astype(F32) + bias_in[None, :]
    value, slope = gelu_parts(pre)
    act, slope = lax.optimization_barrier((value.astype(BF16), slope))
    act_all = lax.all_gather(act, "col", axis=0, tiled=True)

    grad_z = reduce_group(scaled_z, w_out, slope, 0, SPLIT, move_z, move_y)
    grad_y = reduce_group(scaled_y, w_out, slope, SPLIT, hidden - SPLIT, move_y, move_z)
    pieces_z = gather_group(grad_z, move_z, move_y)
    pieces_y = gather_group(grad_y, move_y, move_z)

    in_mine, in_other = row_gather(inputs)
    in_z, in_y = call(
        inputs_kernel,
        [shape((depth, 1024), BF16)] * 2,
        (place, in_mine, in_other),
        "inputs",
        in_specs=[SMEM, VMEM, VMEM],
        out_specs=[VMEM] * 2,
        scratch=[pltpu.VMEM((1024, depth), BF16)] * 2,
    )

    total_z = grad_inputs_group(pieces_z, w_in, 0)
    total_y = grad_inputs_group(pieces_y, w_in, SPLIT)
    send, keep = call(
        join_kernel,
        [shape((512, depth), BF16), shape((512, depth), F32)],
        (place, total_z, total_y),
        "join",
        in_specs=[SMEM, VMEM, VMEM],
        out_specs=[VMEM] * 2,
    )
    keep = keep + swap_core(send).astype(F32)
    parts = [keep[128 * k : 128 * (k + 1)] for k in range(SIDE)]
    grad_inputs = parts[0]
    for k in range(1, SIDE):
        grad_inputs = grad_inputs + move_x(parts[k].astype(BF16), k).astype(F32)

    grad_w_in = grad_w_in_group(in_z, pieces_z, 0, factor, hidden, None)
    grad_w_in = grad_w_in_group(in_y, pieces_y, SPLIT, factor, hidden, grad_w_in)
    grad_w_out = grad_w_out_all(scaled_flipped, act_all, factor)
    return (grad_inputs.astype(BF16), grad_w_in, grad_w_out)


def solution(mesh):
    placed = (
        P("row", "col"),
        P("row", "col"),
        P("col", "row"),
        P("row"),
        P("col", "row"),
        P("row", "col"),
        P(),
    )
    return jax.shard_map(
        shards,
        mesh=mesh,
        in_specs=placed,
        out_specs=(P("row", "col"), P("col", "row"), P("row", "col")),
        check_vma=False,
    )
```

```python
import functools

import jax
import jax.numpy as jnp
from jax import lax
from jax.experimental import pallas as pl
from jax.experimental.pallas import tpu as pltpu
from jax.sharding import PartitionSpec as P

IMAGES = 8
SIDE = 4
BLOCK = 64
WIDE = 512
F32, BF16 = jnp.float32, jnp.bfloat16
NT = (((1,), (1,)), ((), ()))
NN = (((1,), (0,)), ((), ()))


def dot(left, right, dims):
    return lax.dot_general(left, right, dims, preferred_element_type=F32)


def gelu_parts(pre):
    normal_cdf = 0.5 * (1.0 + lax.erf(pre * 0.7071067811865476))
    density = jnp.exp(-0.5 * pre * pre) * 0.3989422804014327
    return (pre * normal_cdf, normal_cdf + pre * density)


def places():
    return [(x, c, y, z) for x in range(SIDE) for c in range(2) for y in range(SIDE) for z in range(SIDE)]


def index(x, c, y, z):
    return (2 * (x % SIDE) + c) * 16 + 4 * (y % SIDE) + z % SIDE


def move(a, by, along_z):
    pairs = [
        (index(x, c, y, z), index(x, c, y, z + by) if c == along_z else index(x, c, y + by, z))
        for x, c, y, z in places()
    ]
    return lax.ppermute(a, ("row", "col"), pairs)


def major(a, by):
    return move(a, by, 0)


def minor(a, by):
    return move(a, by, 1)


def move_x(a, by):
    pairs = [(2 * x + c, 2 * ((x + by) % SIDE) + c) for x in range(SIDE) for c in range(2)]
    return lax.ppermute(a, "row", pairs)


def swap_core(a):
    return lax.ppermute(a, "row", [(2 * x + c, 2 * x + 1 - c) for x in range(SIDE) for c in range(2)])


def call(kernel, outs, operands, name, small=0, order=(), flops=0, scratch=()):
    moved = sum(o.size * o.dtype.itemsize for o in operands) + sum(o.size * o.dtype.itemsize for o in outs)

    def body(*refs):
        kernel(*refs[: len(operands)], *refs[len(operands) + len(order) :])

    return pl.pallas_call(
        body,
        out_shape=outs,
        in_specs=[SMEM] * small + [VMEM] * (len(operands) - small) + [ANY] * len(order),
        out_specs=[VMEM] * len(outs),
        scratch_shapes=scratch,
        name=name,
        cost_estimate=pl.CostEstimate(flops=2 * flops, bytes_accessed=moved, transcendentals=0),
        compiler_params=pltpu.CompilerParams(vmem_limit_bytes=32 * 2**20),
    )(*operands, *order)


def each_block(count, body):
    @pl.loop(0, count // WIDE)
    def _(i):
        body(pl.ds(pl.multiple_of(i * WIDE, WIDE), WIDE))


SMEM = pl.BlockSpec(memory_space=pltpu.SMEM)
VMEM = pl.BlockSpec(memory_space=pltpu.VMEM)
ANY = pl.BlockSpec(memory_space=pl.ANY)


def shape(dims, kind):
    return jax.ShapeDtypeStruct(dims, kind)


def gathered_block(place, mine, other, cols, y, z):
    start = pl.multiple_of(((y - place[2]) & 3) * 128 + (z % 2) * BLOCK, BLOCK)
    rows = pl.ds(start, BLOCK)
    return jnp.where(place[3] == z // 2, mine[rows, cols], other[rows, cols])


def relative(place, y, z):
    dy, dz = (y - place[0]) & 3, (z - place[1]) & 3
    return jnp.where(place[3] == 0, dz, dy), jnp.where(place[3] == 0, dy, dz)


def rows_of(far, near):
    return pl.ds(pl.multiple_of((far * SIDE + near) * BLOCK, BLOCK), BLOCK)


def weight_kernel(lengths, out):
    position = lax.broadcasted_iota(jnp.int32, out.shape, 0)
    size = jnp.zeros(out.shape, jnp.int32)
    start = 0
    for k in range(IMAGES):
        end = start + lengths[k]
        size = jnp.where((position >= start) & (position < end), lengths[k], size)
        start = end
    out[...] = jnp.sqrt(128.0 / size.astype(F32))


def scaled_kernel(place, mine, other, weight, out):
    for y in range(SIDE):
        for z in range(SIDE):
            block = gathered_block(place, mine, other, pl.ds(0, out.shape[1]), y, z)
            here = weight[(y * SIDE + z) * BLOCK : (y * SIDE + z + 1) * BLOCK, :]
            here = jnp.concatenate([here] * (block.shape[1] // 128), axis=1)
            out[rows_of(*relative(place, y, z)), :] = (block.astype(F32) * here).astype(BF16)


def inputs_kernel(place, mine, other, flipped, plain):
    for y in range(SIDE):
        for z in range(SIDE):
            block = gathered_block(place, mine, other, pl.ds(plain.shape[1], plain.shape[1]), y, z)
            plain[rows_of(*relative(place, y, z)), :] = block
    flipped[...] = plain[...].T


def back_kernel(scaled, w, *outs):
    def body(cols):
        total = dot(scaled[...], w[cols, :], NT)
        at = 0
        for out in outs:
            out[:, cols] = total[at : at + out.shape[0]].astype(out.dtype)
            at += out.shape[0]

    each_block(w.shape[0], body)


def back_rows(scaled, w_out, kinds, order=()):
    (rows, depth), hidden = scaled.shape, w_out.shape[0]
    return call(
        back_kernel,
        [shape((count, hidden), kind) for count, kind in kinds],
        (scaled, w_out),
        "back",
        order=order,
        flops=2 * rows * depth * hidden,
    )


def pass_kernel(to_high, to_low, low, high, plus, minus):
    def body(cols):
        plus[:, cols] = (to_high[:, cols] + low[:, cols].astype(F32)).astype(BF16)
        minus[:, cols] = (to_low[:, cols] + high[:, cols].astype(F32)).astype(BF16)

    each_block(plus.shape[1], body)


def sums_kernel(own, low, high, low_sum, high_sum, zero, to_high, plus, minus, to_low):
    def body(cols):
        upper = own[:128, cols] + high[:, cols].astype(F32) + low_sum[:, cols].astype(F32)
        lower = own[128:, cols] + low[:, cols].astype(F32) + high_sum[:, cols].astype(F32)
        zero[:, cols] = upper[:64]
        to_high[:, cols] = upper[64:96]
        plus[:, cols] = jnp.concatenate([upper[96:], lower[:32]], axis=0).astype(BF16)
        minus[:, cols] = lower[32:96].astype(BF16)
        to_low[:, cols] = lower[96:]

    each_block(own.shape[1], body)


def grad_kernel(own, low, high, low_sum, high_sum, slope, grad):
    def body(cols):
        upper = own[:32, cols] + high[32:, cols].astype(F32) + low_sum[:, cols].astype(F32)
        lower = own[32:, cols] + low[:32, cols].astype(F32) + high_sum[:, cols].astype(F32)
        back = jnp.concatenate([upper, lower], axis=0)
        grad[:, cols] = (back * slope[:, cols]).astype(BF16)

    each_block(own.shape[1], body)


def reduce_back(scaled, w_out, order_rest, order_sums):
    hidden = w_out.shape[0]
    half = [(128, BF16)] * 2
    plus, minus = back_rows(scaled[512:768], w_out, half)
    from_low, from_high = major(plus, 1), major(minus, -1)
    beside = jnp.concatenate([scaled[384:512], scaled[768:896]], axis=0)
    plus, minus = back_rows(beside, w_out, half, order_rest)
    low, high = major(plus, 1), major(minus, -1)
    rest = jnp.concatenate([scaled[896:], scaled[:384]], axis=0)
    to_low, own, to_high = back_rows(rest, w_out, [(128, F32), (256, F32), (128, F32)])
    plus, minus = call(pass_kernel, [shape((128, hidden), BF16)] * 2, (to_high, to_low, from_low, from_high), "pass")
    low_sum, high_sum = major(plus, 1), major(minus, -1)
    sums = call(
        sums_kernel,
        [shape((64, hidden), F32), shape((32, hidden), F32)]
        + [shape((64, hidden), BF16)] * 2
        + [shape((32, hidden), F32)],
        (own, low, high, low_sum, high_sum),
        "sums",
        order=order_sums,
    )

    def minor_parts(order):
        zero, to_high, plus, minus, to_low = sums
        low, high = minor(plus, 1), minor(minus, -1)
        plus, minus = call(
            pass_kernel,
            [shape((32, hidden), BF16)] * 2,
            (to_high, to_low, low[32:], high[:32]),
            "pass_minor",
            order=order,
        )
        return zero, low, high, minor(plus, 1), minor(minus, -1)

    return sums, minor_parts


def minor_sides(a):
    return minor(a, 1), minor(a, -1)


def minor_rows(a, low, high):
    return a, high, minor(low[:32], 1), minor(high[32:], -1), low


def stack_kernel(*refs):
    at = 0
    for piece in refs[:-1]:
        refs[-1][at : at + piece.shape[0], :] = piece[...]
        at += piece.shape[0]


def stack(pieces, order=()):
    dims = (sum(p.shape[0] for p in pieces), pieces[0].shape[1])
    return call(stack_kernel, [shape(dims, BF16)], pieces, "stack", order=order)[0]


def grad_inputs_kernel(*refs):
    *pieces, w, out = refs
    at = 0
    for piece in pieces:
        for k in range(0, piece.shape[0], 128):
            out[at : at + 128, :] = dot(piece[k : k + 128, :], w[...], NT)
            at += 128


def grad_inputs_rows(pieces, w_in, name, order=()):
    rows, depth, hidden = sum(p.shape[0] for p in pieces), *w_in.shape
    return call(
        grad_inputs_kernel,
        [shape((rows, depth), F32)],
        (*pieces, w_in),
        name,
        order=order,
        flops=2 * rows * depth * hidden,
    )[0]


def partial_rows(near, far, place, y, z):
    large, small = relative(place, y, z)
    spot = jnp.where(large == 3, 2, jnp.minimum(large, 1))
    return jnp.where(large == 2, far[rows_of(0, small), :], near[rows_of(spot, small), :])


def join_kernel(place, near, far, send, keep):
    for x in range(SIDE):
        for z in range(2):
            for out, core in ((keep, place[3]), (send, 1 - place[3])):
                block = partial_rows(near, far, place, place[2] + x, 2 * core + z)
                out[pl.ds(x * 128 + z * BLOCK, BLOCK), :] = block.astype(out.dtype)


def grad_w_in_kernel(factor, flipped, *refs):
    *pieces, out = refs

    def body(cols):
        rows = jnp.concatenate([piece[:, cols] for piece in pieces], axis=0)
        out[:, cols] = (dot(flipped[...], rows, NN) * factor).astype(BF16)

    each_block(out.shape[1], body)


def grad_w_in_all(flipped, pieces, factor):
    hidden, depth = pieces[0].shape[1], flipped.shape[0]
    return call(
        functools.partial(grad_w_in_kernel, factor),
        [shape((depth, hidden), BF16)],
        (flipped, *pieces),
        "grad_w_in",
        flops=2 * 1024 * depth * hidden,
    )[0]


def flip_kernel(one, two, three, four, five, out):
    def body(cols):
        out[0, cols, :] = jnp.concatenate([one[:, cols], two[:, cols]], axis=0).T
        out[1, cols, :] = jnp.concatenate([three[:, cols], four[:, cols], five[:, cols]], axis=0).T

    each_block(one.shape[1], body)


def flip(rows, order):
    return call(flip_kernel, [shape((2, rows[0].shape[1], 128), BF16)], rows, "flip", order=order)[0]


def grad_w_out_kernel(factor, scaled, one, two, three, four, five, out):
    def body(cols):
        pieces = [p[k, cols, :] for p in (one, two, three, four, five) for k in range(p.shape[0])]
        out[cols, :] = (dot(jnp.concatenate(pieces, axis=1), scaled[...], NN) * factor).astype(BF16)

    each_block(out.shape[0], body)


def grad_w_out_all(scaled, pieces, factor):
    depth, hidden = scaled.shape[1], pieces[0].shape[1]
    return call(
        functools.partial(grad_w_out_kernel, factor),
        [shape((hidden, depth), BF16)],
        (scaled, *pieces),
        "grad_w_out",
        flops=2 * 1024 * depth * hidden,
    )[0]


def beside_kernel(one, two, out):
    depth = one.shape[1]
    out[:, :depth] = one[...]
    out[:, depth:] = two[...]


def row_gather(one, two):
    dims = (one.shape[0], 2 * one.shape[1])
    both = call(beside_kernel, [shape(dims, BF16)], (one, two), "beside")[0]
    mine = stack((both, move_x(both, -1), move_x(both, -2), move_x(both, -3)))
    return mine, swap_core(mine)


def shards(inputs, upstream, preact, bias_in, w_in, w_out, lengths):
    col, row = lax.axis_index("col"), lax.axis_index("row")
    place = jnp.stack([col // SIDE, col % SIDE, row // 2, row % 2]).astype(jnp.int32)
    depth, hidden = w_in.shape
    factor = 1024 ** (-0.5)

    mine, other = row_gather(upstream, inputs)
    weight = call(weight_kernel, [shape((1024, 128), F32)], (lengths,), "weight", small=1)[0]
    pre = preact.astype(F32) + bias_in[None, :]
    value, slope = gelu_parts(pre)
    act, slope = lax.optimization_barrier((value.astype(BF16), slope))
    act_sides = minor_sides(act)
    scaled = call(
        scaled_kernel,
        [shape((1024, depth), BF16)],
        (place, mine, other, weight),
        "scaled",
        small=1,
    )[0]
    act_rows = minor_rows(act, *act_sides)
    sums, minor_parts = reduce_back(scaled, w_out, (), ())
    act_near = flip(act_rows, ())
    act_low, act_high = major(act_near, 1), major(act_near, -1)
    act_pieces = (act_near, act_high, major(act_low[:1], 1), major(act_high[1:], -1), act_low)
    parts = minor_parts(())
    grad = call(grad_kernel, [shape((BLOCK, hidden), BF16)], (*parts, slope), "grad_pre")[0]
    in_flipped = call(
        inputs_kernel,
        [shape((depth, 1024), BF16)],
        (place, mine, other),
        "inputs",
        small=1,
        scratch=[pltpu.VMEM((1024, depth), BF16)],
    )[0]
    grad_w_out = grad_w_out_all(scaled, act_pieces, factor)
    near = stack(minor_rows(grad, *minor_sides(grad)))
    low_a, high_b = major(near[:128], 1), major(near[128:], -1)
    low_b, high_a = major(near[128:], 1), major(near[:128], -1)
    far = major(low_a, 1), major(high_b, -1)
    total_near = grad_inputs_rows((near, high_a, high_b, low_a, low_b), w_in, "grad_inputs_near")
    total_far = grad_inputs_rows(far, w_in, "grad_inputs_far", (total_near, grad_w_out, in_flipped))
    pieces = (near, high_a, high_b, *far, low_a, low_b)
    send, keep = call(
        join_kernel,
        [shape((512, depth), BF16), shape((512, depth), F32)],
        (place, total_near, total_far),
        "join",
        small=1,
    )
    keep = keep + swap_core(send).astype(F32)
    parts = [keep[128 * k : 128 * (k + 1)] for k in range(SIDE)]
    grad_inputs = parts[0]
    for k in range(1, SIDE):
        grad_inputs = grad_inputs + move_x(parts[k].astype(BF16), k).astype(F32)
    grad_w_in = grad_w_in_all(in_flipped, pieces, factor)
    return (grad_inputs.astype(BF16), grad_w_in, grad_w_out)


def solution(mesh):
    placed = (
        P("row", "col"),
        P("row", "col"),
        P("col", "row"),
        P("row"),
        P("col", "row"),
        P("row", "col"),
        P(),
    )
    return jax.shard_map(
        shards,
        mesh=mesh,
        in_specs=placed,
        out_specs=(P("row", "col"), P("col", "row"), P("row", "col")),
        check_vma=False,
    )
```

```python
import functools

import jax
import jax.numpy as jnp
from jax import lax
from jax.experimental import pallas as pl
from jax.experimental.pallas import tpu as pltpu
from jax.sharding import PartitionSpec as P

IMAGES = 8
SIDE = 4
BLOCK = 64
WIDE = 512
F32, BF16 = jnp.float32, jnp.bfloat16
NT = (((1,), (1,)), ((), ()))
NN = (((1,), (0,)), ((), ()))


def dot(left, right, dims):
    return lax.dot_general(left, right, dims, preferred_element_type=F32)


def gelu_parts(pre):
    normal_cdf = 0.5 * (1.0 + lax.erf(pre * 0.7071067811865476))
    density = jnp.exp(-0.5 * pre * pre) * 0.3989422804014327
    return (pre * normal_cdf, normal_cdf + pre * density)


def places():
    return [(x, c, y, z) for x in range(SIDE) for c in range(2) for y in range(SIDE) for z in range(SIDE)]


def index(x, c, y, z):
    return (2 * (x % SIDE) + c) * 16 + 4 * (y % SIDE) + z % SIDE


def move(a, by, along_z):
    pairs = [
        (index(x, c, y, z), index(x, c, y, z + by) if c == along_z else index(x, c, y + by, z))
        for x, c, y, z in places()
    ]
    return lax.ppermute(a, ("row", "col"), pairs)


def major(a, by):
    return move(a, by, 0)


def minor(a, by):
    return move(a, by, 1)


def move_x(a, by):
    pairs = [(2 * x + c, 2 * ((x + by) % SIDE) + c) for x in range(SIDE) for c in range(2)]
    return lax.ppermute(a, "row", pairs)


def swap_core(a):
    return lax.ppermute(a, "row", [(2 * x + c, 2 * x + 1 - c) for x in range(SIDE) for c in range(2)])


def call(kernel, outs, operands, name, small=0, order=(), flops=0, scratch=()):
    moved = sum(o.size * o.dtype.itemsize for o in operands) + sum(o.size * o.dtype.itemsize for o in outs)

    def body(*refs):
        kernel(*refs[: len(operands)], *refs[len(operands) + len(order) :])

    return pl.pallas_call(
        body,
        out_shape=outs,
        in_specs=[SMEM] * small + [VMEM] * (len(operands) - small) + [ANY] * len(order),
        out_specs=[VMEM] * len(outs),
        scratch_shapes=scratch,
        name=name,
        cost_estimate=pl.CostEstimate(flops=0, bytes_accessed=0, transcendentals=0),
        compiler_params=pltpu.CompilerParams(vmem_limit_bytes=32 * 2**20),
    )(*operands, *order)


def each_block(count, body):
    @pl.loop(0, count // WIDE)
    def _(i):
        body(pl.ds(pl.multiple_of(i * WIDE, WIDE), WIDE))


SMEM = pl.BlockSpec(memory_space=pltpu.SMEM)
VMEM = pl.BlockSpec(memory_space=pltpu.VMEM)
ANY = pl.BlockSpec(memory_space=pl.ANY)


def shape(dims, kind):
    return jax.ShapeDtypeStruct(dims, kind)


def gathered_block(place, mine, other, y, z):
    start = pl.multiple_of(((y - place[2]) & 3) * 128 + (z % 2) * BLOCK, BLOCK)
    rows = pl.ds(start, BLOCK)
    return jnp.where(place[3] == z // 2, mine[rows, :], other[rows, :])


def relative(place, y, z):
    dy, dz = (y - place[0]) & 3, (z - place[1]) & 3
    return jnp.where(place[3] == 0, dz, dy), jnp.where(place[3] == 0, dy, dz)


def rows_of(far, near):
    return pl.ds(pl.multiple_of((far * SIDE + near) * BLOCK, BLOCK), BLOCK)


def weight_kernel(lengths, out):
    position = lax.broadcasted_iota(jnp.int32, out.shape, 0)
    size = jnp.zeros(out.shape, jnp.int32)
    start = 0
    for k in range(IMAGES):
        end = start + lengths[k]
        size = jnp.where((position >= start) & (position < end), lengths[k], size)
        start = end
    out[...] = jnp.sqrt(128.0 / size.astype(F32))


def scaled_kernel(place, mine, other, weight, out):
    for y in range(SIDE):
        for z in range(SIDE):
            block = gathered_block(place, mine, other, y, z)
            here = weight[(y * SIDE + z) * BLOCK : (y * SIDE + z + 1) * BLOCK, :]
            here = jnp.concatenate([here] * (block.shape[1] // 128), axis=1)
            out[rows_of(*relative(place, y, z)), :] = (block.astype(F32) * here).astype(BF16)


def inputs_kernel(place, mine, other, flipped, plain):
    for y in range(SIDE):
        for z in range(SIDE):
            plain[rows_of(*relative(place, y, z)), :] = gathered_block(place, mine, other, y, z)
    flipped[...] = plain[...].T


def back_kernel(scaled, w, *outs):
    def body(cols):
        total = dot(scaled[...], w[cols, :], NT)
        at = 0
        for out in outs:
            out[:, cols] = total[at : at + out.shape[0]].astype(out.dtype)
            at += out.shape[0]

    each_block(w.shape[0], body)


def back_rows(scaled, w_out, kinds, order=()):
    (rows, depth), hidden = scaled.shape, w_out.shape[0]
    return call(
        back_kernel,
        [shape((count, hidden), kind) for count, kind in kinds],
        (scaled, w_out),
        "back",
        order=order,
        flops=2 * rows * depth * hidden,
    )


def pass_kernel(to_high, to_low, low, high, plus, minus):
    def body(cols):
        plus[:, cols] = (to_high[:, cols] + low[:, cols].astype(F32)).astype(BF16)
        minus[:, cols] = (to_low[:, cols] + high[:, cols].astype(F32)).astype(BF16)

    each_block(plus.shape[1], body)


def sums_kernel(own, low, high, low_sum, high_sum, zero, to_high, plus, minus, to_low):
    def body(cols):
        upper = own[:128, cols] + high[:, cols].astype(F32) + low_sum[:, cols].astype(F32)
        lower = own[128:, cols] + low[:, cols].astype(F32) + high_sum[:, cols].astype(F32)
        zero[:, cols] = upper[:64]
        to_high[:, cols] = upper[64:96]
        plus[:, cols] = jnp.concatenate([upper[96:], lower[:32]], axis=0).astype(BF16)
        minus[:, cols] = lower[32:96].astype(BF16)
        to_low[:, cols] = lower[96:]

    each_block(own.shape[1], body)


def grad_kernel(own, low, high, low_sum, high_sum, slope, grad):
    def body(cols):
        upper = own[:32, cols] + high[32:, cols].astype(F32) + low_sum[:, cols].astype(F32)
        lower = own[32:, cols] + low[:32, cols].astype(F32) + high_sum[:, cols].astype(F32)
        back = jnp.concatenate([upper, lower], axis=0)
        grad[:, cols] = (back * slope[:, cols]).astype(BF16)

    each_block(own.shape[1], body)


def reduce_back(scaled, w_out, order_rest, order_sums):
    hidden = w_out.shape[0]
    half = [(128, BF16)] * 2
    plus, minus = back_rows(scaled[512:768], w_out, half)
    from_low, from_high = major(plus, 1), major(minus, -1)
    rest = jnp.concatenate([scaled[768:], scaled[:512]], axis=0)
    minus, to_low, own, to_high, plus = back_rows(
        rest, w_out, [(128, BF16), (128, F32), (256, F32), (128, F32), (128, BF16)], order_rest
    )
    low, high = major(plus, 1), major(minus, -1)
    plus, minus = call(pass_kernel, [shape((128, hidden), BF16)] * 2, (to_high, to_low, from_low, from_high), "pass")
    low_sum, high_sum = major(plus, 1), major(minus, -1)
    sums = call(
        sums_kernel,
        [shape((64, hidden), F32), shape((32, hidden), F32)]
        + [shape((64, hidden), BF16)] * 2
        + [shape((32, hidden), F32)],
        (own, low, high, low_sum, high_sum),
        "sums",
        order=order_sums,
    )

    def minor_parts(order):
        zero, to_high, plus, minus, to_low = sums
        low, high = minor(plus, 1), minor(minus, -1)
        plus, minus = call(
            pass_kernel,
            [shape((32, hidden), BF16)] * 2,
            (to_high, to_low, low[32:], high[:32]),
            "pass_minor",
            order=order,
        )
        return zero, low, high, minor(plus, 1), minor(minus, -1)

    return sums, minor_parts


def minor_sides(a):
    return minor(a, 1), minor(a, -1)


def minor_rows(a, low, high):
    return a, high, minor(low[:32], 1), minor(high[32:], -1), low


def stack_kernel(*refs):
    at = 0
    for piece in refs[:-1]:
        refs[-1][at : at + piece.shape[0], :] = piece[...]
        at += piece.shape[0]


def stack(pieces, order=()):
    dims = (sum(p.shape[0] for p in pieces), pieces[0].shape[1])
    return call(stack_kernel, [shape(dims, BF16)], pieces, "stack", order=order)[0]


def grad_inputs_kernel(*refs):
    *pieces, w, out = refs
    at = 0
    for piece in pieces:
        for k in range(0, piece.shape[0], 128):
            out[at : at + 128, :] = dot(piece[k : k + 128, :], w[...], NT)
            at += 128


def grad_inputs_rows(pieces, w_in, name, order=()):
    rows, depth, hidden = sum(p.shape[0] for p in pieces), *w_in.shape
    return call(
        grad_inputs_kernel,
        [shape((rows, depth), F32)],
        (*pieces, w_in),
        name,
        order=order,
        flops=2 * rows * depth * hidden,
    )[0]


def partial_rows(near, far, place, y, z):
    large, small = relative(place, y, z)
    spot = jnp.where(large == 3, 2, jnp.minimum(large, 1))
    return jnp.where(large == 2, far[rows_of(0, small), :], near[rows_of(spot, small), :])


def join_kernel(place, near, far, send, keep):
    for x in range(SIDE):
        for z in range(2):
            for out, core in ((keep, place[3]), (send, 1 - place[3])):
                block = partial_rows(near, far, place, place[2] + x, 2 * core + z)
                out[pl.ds(x * 128 + z * BLOCK, BLOCK), :] = block.astype(out.dtype)


def grad_w_in_kernel(factor, flipped, *refs):
    *pieces, out = refs

    def body(cols):
        rows = jnp.concatenate([piece[:, cols] for piece in pieces], axis=0)
        out[:, cols] = (dot(flipped[...], rows, NN) * factor).astype(BF16)

    each_block(out.shape[1], body)


def grad_w_in_all(flipped, pieces, factor):
    hidden, depth = pieces[0].shape[1], flipped.shape[0]
    return call(
        functools.partial(grad_w_in_kernel, factor),
        [shape((depth, hidden), BF16)],
        (flipped, *pieces),
        "grad_w_in",
        flops=2 * 1024 * depth * hidden,
    )[0]


def flip_kernel(one, two, three, four, five, out):
    def body(cols):
        out[0, cols, :] = jnp.concatenate([one[:, cols], two[:, cols]], axis=0).T
        out[1, cols, :] = jnp.concatenate([three[:, cols], four[:, cols], five[:, cols]], axis=0).T

    each_block(one.shape[1], body)


def flip(rows, order):
    return call(flip_kernel, [shape((2, rows[0].shape[1], 128), BF16)], rows, "flip", order=order)[0]


def grad_w_out_kernel(factor, scaled, one, two, three, four, five, out):
    def body(cols):
        pieces = [p[k, cols, :] for p in (one, two, three, four, five) for k in range(p.shape[0])]
        out[cols, :] = (dot(jnp.concatenate(pieces, axis=1), scaled[...], NN) * factor).astype(BF16)

    each_block(out.shape[0], body)


def grad_w_out_all(scaled, pieces, factor):
    depth, hidden = scaled.shape[1], pieces[0].shape[1]
    return call(
        functools.partial(grad_w_out_kernel, factor),
        [shape((hidden, depth), BF16)],
        (scaled, *pieces),
        "grad_w_out",
        flops=2 * 1024 * depth * hidden,
    )[0]


def row_gather(a):
    mine = stack((a, move_x(a, -1), move_x(a, -2), move_x(a, -3)))
    return mine, swap_core(mine)


def hold_kernel(a, out):
    out[...] = a[...]


def hold(a, order):
    return call(hold_kernel, [shape(a.shape, a.dtype)], (a,), "hold", order=order)[0]


def shards(inputs, upstream, preact, bias_in, w_in, w_out, lengths):
    col, row = lax.axis_index("col"), lax.axis_index("row")
    place = jnp.stack([col // SIDE, col % SIDE, row // 2, row % 2]).astype(jnp.int32)
    depth, hidden = w_in.shape
    factor = 1024 ** (-0.5)

    up_mine, up_other = row_gather(upstream)
    weight = call(weight_kernel, [shape((1024, 128), F32)], (lengths,), "weight", small=1)[0]
    pre = preact.astype(F32) + bias_in[None, :]
    value, slope = gelu_parts(pre)
    act, slope = lax.optimization_barrier((value.astype(BF16), slope))
    act_sides = minor_sides(act)
    scaled = call(
        scaled_kernel,
        [shape((1024, depth), BF16)],
        (place, up_mine, up_other, weight),
        "scaled",
        small=1,
        order=act_sides,
    )[0]
    act_rows = minor_rows(act, *act_sides)
    in_mine, in_other = row_gather(hold(inputs, (up_mine,)))
    in_flipped = call(
        inputs_kernel,
        [shape((depth, 1024), BF16)],
        (place, in_mine, in_other),
        "inputs",
        small=1,
        scratch=[pltpu.VMEM((1024, depth), BF16)],
    )[0]
    sums, minor_parts = reduce_back(scaled, w_out, (), act_rows)
    act_near = flip(act_rows, sums[:1])
    act_low, act_high = major(act_near, 1), major(act_near, -1)
    act_pieces = (act_near, act_high, major(act_low[:1], 1), major(act_high[1:], -1), act_low)

    parts = minor_parts((act_near,))
    grad = call(grad_kernel, [shape((BLOCK, hidden), BF16)], (*parts, slope), "grad_pre", order=(act_low, act_high))[0]
    grad_w_out = grad_w_out_all(scaled, act_pieces, factor)
    near = stack(minor_rows(grad, *minor_sides(grad)), (*act_pieces[2:4], in_flipped))
    low_a, high_b = major(near[:128], 1), major(near[128:], -1)
    low_b, high_a = major(near[128:], 1), major(near[:128], -1)
    far = major(low_a, 1), major(high_b, -1)
    total_near = grad_inputs_rows((near, high_a, high_b, low_a, low_b), w_in, "grad_inputs_near")
    total_far = grad_inputs_rows(far, w_in, "grad_inputs_far", (total_near, grad_w_out))
    pieces = (near, high_a, high_b, *far, low_a, low_b)
    send, keep = call(
        join_kernel,
        [shape((512, depth), BF16), shape((512, depth), F32)],
        (place, total_near, total_far),
        "join",
        small=1,
    )
    keep = keep + swap_core(send).astype(F32)
    parts = [keep[128 * k : 128 * (k + 1)] for k in range(SIDE)]
    grad_inputs = parts[0]
    for k in range(1, SIDE):
        grad_inputs = grad_inputs + move_x(parts[k].astype(BF16), k).astype(F32)
    grad_w_in = grad_w_in_all(in_flipped, pieces, factor)
    return (grad_inputs.astype(BF16), grad_w_in, grad_w_out)


def solution(mesh):
    placed = (
        P("row", "col"),
        P("row", "col"),
        P("col", "row"),
        P("row"),
        P("col", "row"),
        P("row", "col"),
        P(),
    )
    return jax.shard_map(
        shards,
        mesh=mesh,
        in_specs=placed,
        out_specs=(P("row", "col"), P("col", "row"), P("row", "col")),
        check_vma=False,
    )
```

```python
import functools

import jax
import jax.numpy as jnp
from jax import lax
from jax.experimental import pallas as pl
from jax.experimental.pallas import tpu as pltpu
from jax.sharding import PartitionSpec as P

IMAGES = 8
SIDE = 4
BLOCK = 64
WIDE = 512
F32, BF16 = jnp.float32, jnp.bfloat16
NT = (((1,), (1,)), ((), ()))
NN = (((1,), (0,)), ((), ()))


def dot(left, right, dims):
    return lax.dot_general(left, right, dims, preferred_element_type=F32)


def gelu_parts(pre):
    normal_cdf = 0.5 * (1.0 + lax.erf(pre * 0.7071067811865476))
    density = jnp.exp(-0.5 * pre * pre) * 0.3989422804014327
    return (pre * normal_cdf, normal_cdf + pre * density)


def places():
    return [(x, c, y, z) for x in range(SIDE) for c in range(2) for y in range(SIDE) for z in range(SIDE)]


def index(x, c, y, z):
    return (2 * (x % SIDE) + c) * 16 + 4 * (y % SIDE) + z % SIDE


def move(a, by, along_z):
    pairs = [
        (index(x, c, y, z), index(x, c, y, z + by) if c == along_z else index(x, c, y + by, z))
        for x, c, y, z in places()
    ]
    return lax.ppermute(a, ("row", "col"), pairs)


def major(a, by):
    return move(a, by, 0)


def minor(a, by):
    return move(a, by, 1)


def move_x(a, by):
    pairs = [(2 * x + c, 2 * ((x + by) % SIDE) + c) for x in range(SIDE) for c in range(2)]
    return lax.ppermute(a, "row", pairs)


def swap_core(a):
    return lax.ppermute(a, "row", [(2 * x + c, 2 * x + 1 - c) for x in range(SIDE) for c in range(2)])


def call(kernel, outs, operands, name, small=0, order=(), flops=0, scratch=()):
    moved = sum(o.size * o.dtype.itemsize for o in operands) + sum(o.size * o.dtype.itemsize for o in outs)

    def body(*refs):
        kernel(*refs[: len(operands)], *refs[len(operands) + len(order) :])

    return pl.pallas_call(
        body,
        out_shape=outs,
        in_specs=[SMEM] * small + [VMEM] * (len(operands) - small) + [ANY] * len(order),
        out_specs=[VMEM] * len(outs),
        scratch_shapes=scratch,
        name=name,
        cost_estimate=pl.CostEstimate(flops=0, bytes_accessed=0, transcendentals=0),
        compiler_params=pltpu.CompilerParams(vmem_limit_bytes=32 * 2**20),
    )(*operands, *order)


def each_block(count, body):
    @pl.loop(0, count // WIDE)
    def _(i):
        body(pl.ds(pl.multiple_of(i * WIDE, WIDE), WIDE))


SMEM = pl.BlockSpec(memory_space=pltpu.SMEM)
VMEM = pl.BlockSpec(memory_space=pltpu.VMEM)
ANY = pl.BlockSpec(memory_space=pl.ANY)


def shape(dims, kind):
    return jax.ShapeDtypeStruct(dims, kind)


def gathered_block(place, mine, other, y, z):
    start = pl.multiple_of(((y - place[2]) & 3) * 128 + (z % 2) * BLOCK, BLOCK)
    rows = pl.ds(start, BLOCK)
    return jnp.where(place[3] == z // 2, mine[rows, :], other[rows, :])


def relative(place, y, z):
    dy, dz = (y - place[0]) & 3, (z - place[1]) & 3
    return jnp.where(place[3] == 0, dz, dy), jnp.where(place[3] == 0, dy, dz)


def rows_of(far, near):
    return pl.ds(pl.multiple_of((far * SIDE + near) * BLOCK, BLOCK), BLOCK)


def weight_kernel(lengths, out):
    position = lax.broadcasted_iota(jnp.int32, out.shape, 0)
    size = jnp.zeros(out.shape, jnp.int32)
    start = 0
    for k in range(IMAGES):
        end = start + lengths[k]
        size = jnp.where((position >= start) & (position < end), lengths[k], size)
        start = end
    out[...] = jnp.sqrt(128.0 / size.astype(F32))


def scaled_kernel(place, mine, other, weight, out):
    for y in range(SIDE):
        for z in range(SIDE):
            block = gathered_block(place, mine, other, y, z)
            here = weight[(y * SIDE + z) * BLOCK : (y * SIDE + z + 1) * BLOCK, :]
            here = jnp.concatenate([here] * (block.shape[1] // 128), axis=1)
            out[rows_of(*relative(place, y, z)), :] = (block.astype(F32) * here).astype(BF16)


def inputs_kernel(place, mine, other, flipped, plain):
    for y in range(SIDE):
        for z in range(SIDE):
            plain[rows_of(*relative(place, y, z)), :] = gathered_block(place, mine, other, y, z)
    flipped[...] = plain[...].T


def back_kernel(scaled, w, *outs):
    def body(cols):
        total = dot(scaled[...], w[cols, :], NT)
        at = 0
        for out in outs:
            out[:, cols] = total[at : at + out.shape[0]].astype(out.dtype)
            at += out.shape[0]

    each_block(w.shape[0], body)


def back_rows(scaled, w_out, kinds, order=()):
    (rows, depth), hidden = scaled.shape, w_out.shape[0]
    return call(
        back_kernel,
        [shape((count, hidden), kind) for count, kind in kinds],
        (scaled, w_out),
        "back",
        order=order,
        flops=2 * rows * depth * hidden,
    )


def pass_kernel(to_high, to_low, low, high, plus, minus):
    def body(cols):
        plus[:, cols] = (to_high[:, cols] + low[:, cols].astype(F32)).astype(BF16)
        minus[:, cols] = (to_low[:, cols] + high[:, cols].astype(F32)).astype(BF16)

    each_block(plus.shape[1], body)


def sums_kernel(own, low, high, low_sum, high_sum, zero, to_high, plus, minus, to_low):
    def body(cols):
        upper = own[:128, cols] + high[:, cols].astype(F32) + low_sum[:, cols].astype(F32)
        lower = own[128:, cols] + low[:, cols].astype(F32) + high_sum[:, cols].astype(F32)
        zero[:, cols] = upper[:64]
        to_high[:, cols] = upper[64:96]
        plus[:, cols] = jnp.concatenate([upper[96:], lower[:32]], axis=0).astype(BF16)
        minus[:, cols] = lower[32:96].astype(BF16)
        to_low[:, cols] = lower[96:]

    each_block(own.shape[1], body)


def grad_kernel(own, low, high, low_sum, high_sum, slope, grad):
    def body(cols):
        upper = own[:32, cols] + high[32:, cols].astype(F32) + low_sum[:, cols].astype(F32)
        lower = own[32:, cols] + low[:32, cols].astype(F32) + high_sum[:, cols].astype(F32)
        back = jnp.concatenate([upper, lower], axis=0)
        grad[:, cols] = (back * slope[:, cols]).astype(BF16)

    each_block(own.shape[1], body)


def reduce_back(scaled, w_out, order_rest, order_sums):
    hidden = w_out.shape[0]
    half = [(128, BF16)] * 2
    plus, minus = back_rows(scaled[512:768], w_out, half)
    from_low, from_high = major(plus, 1), major(minus, -1)
    rest = jnp.concatenate([scaled[768:], scaled[:512]], axis=0)
    minus, to_low, own, to_high, plus = back_rows(
        rest, w_out, [(128, BF16), (128, F32), (256, F32), (128, F32), (128, BF16)], order_rest
    )
    low, high = major(plus, 1), major(minus, -1)
    plus, minus = call(pass_kernel, [shape((128, hidden), BF16)] * 2, (to_high, to_low, from_low, from_high), "pass")
    low_sum, high_sum = major(plus, 1), major(minus, -1)
    sums = call(
        sums_kernel,
        [shape((64, hidden), F32), shape((32, hidden), F32)]
        + [shape((64, hidden), BF16)] * 2
        + [shape((32, hidden), F32)],
        (own, low, high, low_sum, high_sum),
        "sums",
        order=order_sums,
    )

    def minor_parts(order):
        zero, to_high, plus, minus, to_low = sums
        low, high = minor(plus, 1), minor(minus, -1)
        plus, minus = call(
            pass_kernel,
            [shape((32, hidden), BF16)] * 2,
            (to_high, to_low, low[32:], high[:32]),
            "pass_minor",
            order=order,
        )
        return zero, low, high, minor(plus, 1), minor(minus, -1)

    return sums, minor_parts


def minor_sides(a):
    return minor(a, 1), minor(a, -1)


def minor_rows(a, low, high):
    return a, high, minor(low[:32], 1), minor(high[32:], -1), low


def stack_kernel(*refs):
    at = 0
    for piece in refs[:-1]:
        refs[-1][at : at + piece.shape[0], :] = piece[...]
        at += piece.shape[0]


def stack(pieces, order=()):
    dims = (sum(p.shape[0] for p in pieces), pieces[0].shape[1])
    return call(stack_kernel, [shape(dims, BF16)], pieces, "stack", order=order)[0]


def grad_inputs_kernel(*refs):
    *pieces, w, out = refs
    at = 0
    for piece in pieces:
        for k in range(0, piece.shape[0], 128):
            out[at : at + 128, :] = dot(piece[k : k + 128, :], w[...], NT)
            at += 128


def grad_inputs_rows(pieces, w_in, name, order=()):
    rows, depth, hidden = sum(p.shape[0] for p in pieces), *w_in.shape
    return call(
        grad_inputs_kernel,
        [shape((rows, depth), F32)],
        (*pieces, w_in),
        name,
        order=order,
        flops=2 * rows * depth * hidden,
    )[0]


def partial_rows(near, far, place, y, z):
    large, small = relative(place, y, z)
    spot = jnp.where(large == 3, 2, jnp.minimum(large, 1))
    return jnp.where(large == 2, far[rows_of(0, small), :], near[rows_of(spot, small), :])


def join_kernel(place, near, far, send, keep):
    for x in range(SIDE):
        for z in range(2):
            for out, core in ((keep, place[3]), (send, 1 - place[3])):
                block = partial_rows(near, far, place, place[2] + x, 2 * core + z)
                out[pl.ds(x * 128 + z * BLOCK, BLOCK), :] = block.astype(out.dtype)


def grad_w_in_kernel(factor, flipped, *refs):
    *pieces, out = refs

    def body(cols):
        rows = jnp.concatenate([piece[:, cols] for piece in pieces], axis=0)
        out[:, cols] = (dot(flipped[...], rows, NN) * factor).astype(BF16)

    each_block(out.shape[1], body)


def grad_w_in_all(flipped, pieces, factor):
    hidden, depth = pieces[0].shape[1], flipped.shape[0]
    return call(
        functools.partial(grad_w_in_kernel, factor),
        [shape((depth, hidden), BF16)],
        (flipped, *pieces),
        "grad_w_in",
        flops=2 * 1024 * depth * hidden,
    )[0]


def flip_kernel(one, two, three, four, five, out):
    def body(cols):
        out[0, cols, :] = jnp.concatenate([one[:, cols], two[:, cols]], axis=0).T
        out[1, cols, :] = jnp.concatenate([three[:, cols], four[:, cols], five[:, cols]], axis=0).T

    each_block(one.shape[1], body)


def flip(rows, order):
    return call(flip_kernel, [shape((2, rows[0].shape[1], 128), BF16)], rows, "flip", order=order)[0]


def grad_w_out_kernel(factor, scaled, one, two, three, four, five, out):
    def body(cols):
        pieces = [p[k, cols, :] for p in (one, two, three, four, five) for k in range(p.shape[0])]
        out[cols, :] = (dot(jnp.concatenate(pieces, axis=1), scaled[...], NN) * factor).astype(BF16)

    each_block(out.shape[0], body)


def grad_w_out_all(scaled, pieces, factor):
    depth, hidden = scaled.shape[1], pieces[0].shape[1]
    return call(
        functools.partial(grad_w_out_kernel, factor),
        [shape((hidden, depth), BF16)],
        (scaled, *pieces),
        "grad_w_out",
        flops=2 * 1024 * depth * hidden,
    )[0]


def row_gather(a):
    mine = stack((a, move_x(a, -1), move_x(a, -2), move_x(a, -3)))
    return mine, swap_core(mine)


def hold_kernel(a, out):
    out[...] = a[...]


def hold(a, order):
    return call(hold_kernel, [shape(a.shape, a.dtype)], (a,), "hold", order=order)[0]


def shards(inputs, upstream, preact, bias_in, w_in, w_out, lengths):
    col, row = lax.axis_index("col"), lax.axis_index("row")
    place = jnp.stack([col // SIDE, col % SIDE, row // 2, row % 2]).astype(jnp.int32)
    depth, hidden = w_in.shape
    factor = 1024 ** (-0.5)

    up_mine, up_other = row_gather(upstream)
    weight = call(weight_kernel, [shape((1024, 128), F32)], (lengths,), "weight", small=1)[0]
    pre = preact.astype(F32) + bias_in[None, :]
    value, slope = gelu_parts(pre)
    act, slope = lax.optimization_barrier((value.astype(BF16), slope))
    act_sides = minor_sides(act)
    scaled = call(
        scaled_kernel,
        [shape((1024, depth), BF16)],
        (place, up_mine, up_other, weight),
        "scaled",
        small=1,
        order=act_sides[:1],
    )[0]
    act_rows = minor_rows(act, *act_sides)
    in_mine, in_other = row_gather(hold(inputs, (up_mine,)))
    in_flipped = call(
        inputs_kernel,
        [shape((depth, 1024), BF16)],
        (place, in_mine, in_other),
        "inputs",
        small=1,
        scratch=[pltpu.VMEM((1024, depth), BF16)],
    )[0]
    sums, minor_parts = reduce_back(scaled, w_out, (), act_rows)
    act_near = flip(act_rows, sums[:1])
    act_low, act_high = major(act_near, 1), major(act_near, -1)
    act_pieces = (act_near, act_high, major(act_low[:1], 1), major(act_high[1:], -1), act_low)

    parts = minor_parts((act_near,))
    grad = call(grad_kernel, [shape((BLOCK, hidden), BF16)], (*parts, slope), "grad_pre", order=(act_low, act_high))[0]
    grad_w_out = grad_w_out_all(scaled, act_pieces, factor)
    near = stack(minor_rows(grad, *minor_sides(grad)), (*act_pieces[2:4], in_flipped))
    low_a, high_b = major(near[:128], 1), major(near[128:], -1)
    low_b, high_a = major(near[128:], 1), major(near[:128], -1)
    far = major(low_a, 1), major(high_b, -1)
    total_near = grad_inputs_rows((near, high_a, high_b, low_a, low_b), w_in, "grad_inputs_near")
    total_far = grad_inputs_rows(far, w_in, "grad_inputs_far", (total_near, grad_w_out))
    pieces = (near, high_a, high_b, *far, low_a, low_b)
    send, keep = call(
        join_kernel,
        [shape((512, depth), BF16), shape((512, depth), F32)],
        (place, total_near, total_far),
        "join",
        small=1,
    )
    keep = keep + swap_core(send).astype(F32)
    parts = [keep[128 * k : 128 * (k + 1)] for k in range(SIDE)]
    grad_inputs = parts[0]
    for k in range(1, SIDE):
        grad_inputs = grad_inputs + move_x(parts[k].astype(BF16), k).astype(F32)
    grad_w_in = grad_w_in_all(in_flipped, pieces, factor)
    return (grad_inputs.astype(BF16), grad_w_in, grad_w_out)


def solution(mesh):
    placed = (
        P("row", "col"),
        P("row", "col"),
        P("col", "row"),
        P("row"),
        P("col", "row"),
        P("row", "col"),
        P(),
    )
    return jax.shard_map(
        shards,
        mesh=mesh,
        in_specs=placed,
        out_specs=(P("row", "col"), P("col", "row"), P("row", "col")),
        check_vma=False,
    )
```

```python
import functools

import jax
import jax.numpy as jnp
from jax import lax
from jax.experimental import pallas as pl
from jax.experimental.pallas import tpu as pltpu
from jax.sharding import PartitionSpec as P

IMAGES = 8
SIDE = 4
BLOCK = 64
WIDE = 512
F32, BF16 = jnp.float32, jnp.bfloat16
NT = (((1,), (1,)), ((), ()))
NN = (((1,), (0,)), ((), ()))


def dot(left, right, dims):
    return lax.dot_general(left, right, dims, preferred_element_type=F32)


def gelu_parts(pre):
    normal_cdf = 0.5 * (1.0 + lax.erf(pre * 0.7071067811865476))
    density = jnp.exp(-0.5 * pre * pre) * 0.3989422804014327
    return (pre * normal_cdf, normal_cdf + pre * density)


def places():
    return [(x, c, y, z) for x in range(SIDE) for c in range(2) for y in range(SIDE) for z in range(SIDE)]


def index(x, c, y, z):
    return (2 * (x % SIDE) + c) * 16 + 4 * (y % SIDE) + z % SIDE


def move(a, by, along_z):
    pairs = [
        (index(x, c, y, z), index(x, c, y, z + by) if c == along_z else index(x, c, y + by, z))
        for x, c, y, z in places()
    ]
    return lax.ppermute(a, ("row", "col"), pairs)


def major(a, by):
    return move(a, by, 0)


def minor(a, by):
    return move(a, by, 1)


def move_x(a, by):
    pairs = [(2 * x + c, 2 * ((x + by) % SIDE) + c) for x in range(SIDE) for c in range(2)]
    return lax.ppermute(a, "row", pairs)


def swap_core(a):
    return lax.ppermute(a, "row", [(2 * x + c, 2 * x + 1 - c) for x in range(SIDE) for c in range(2)])


def call(kernel, outs, operands, name, small=0, order=(), flops=0, scratch=()):
    moved = sum(o.size * o.dtype.itemsize for o in operands) + sum(o.size * o.dtype.itemsize for o in outs)

    def body(*refs):
        kernel(*refs[: len(operands)], *refs[len(operands) + len(order) :])

    return pl.pallas_call(
        body,
        out_shape=outs,
        in_specs=[SMEM] * small + [VMEM] * (len(operands) - small) + [ANY] * len(order),
        out_specs=[VMEM] * len(outs),
        scratch_shapes=scratch,
        name=name,
        cost_estimate=pl.CostEstimate(flops=0, bytes_accessed=0, transcendentals=0),
        compiler_params=pltpu.CompilerParams(vmem_limit_bytes=32 * 2**20),
    )(*operands, *order)


def each_block(count, body, wide=WIDE):
    @pl.loop(0, count // wide)
    def _(i):
        body(pl.ds(pl.multiple_of(i * wide, wide), wide))


SMEM = pl.BlockSpec(memory_space=pltpu.SMEM)
VMEM = pl.BlockSpec(memory_space=pltpu.VMEM)
ANY = pl.BlockSpec(memory_space=pl.ANY)


def shape(dims, kind):
    return jax.ShapeDtypeStruct(dims, kind)


def gathered_block(place, mine, other, y, z):
    start = pl.multiple_of(((y - place[2]) & 3) * 128 + (z % 2) * BLOCK, BLOCK)
    rows = pl.ds(start, BLOCK)
    return jnp.where(place[3] == z // 2, mine[rows, :], other[rows, :])


def relative(place, y, z):
    dy, dz = (y - place[0]) & 3, (z - place[1]) & 3
    return jnp.where(place[3] == 0, dz, dy), jnp.where(place[3] == 0, dy, dz)


def rows_of(far, near):
    return pl.ds(pl.multiple_of((far * SIDE + near) * BLOCK, BLOCK), BLOCK)


def weight_kernel(lengths, out):
    position = lax.broadcasted_iota(jnp.int32, out.shape, 0)
    size = jnp.zeros(out.shape, jnp.int32)
    start = 0
    for k in range(IMAGES):
        end = start + lengths[k]
        size = jnp.where((position >= start) & (position < end), lengths[k], size)
        start = end
    out[...] = jnp.sqrt(128.0 / size.astype(F32))


def scaled_kernel(place, mine, other, weight, out):
    for y in range(SIDE):
        for z in range(SIDE):
            block = gathered_block(place, mine, other, y, z)
            here = weight[(y * SIDE + z) * BLOCK : (y * SIDE + z + 1) * BLOCK, :]
            here = jnp.concatenate([here] * (block.shape[1] // 128), axis=1)
            out[rows_of(*relative(place, y, z)), :] = (block.astype(F32) * here).astype(BF16)


def inputs_kernel(place, mine, other, flipped, plain):
    for y in range(SIDE):
        for z in range(SIDE):
            plain[rows_of(*relative(place, y, z)), :] = gathered_block(place, mine, other, y, z)
    flipped[...] = plain[...].T


def back_kernel(scaled, w, *outs):
    def body(cols):
        total = dot(scaled[...], w[cols, :], NT)
        at = 0
        for out in outs:
            out[:, cols] = total[at : at + out.shape[0]].astype(out.dtype)
            at += out.shape[0]

    each_block(w.shape[0], body, 2 * WIDE)


def back_rows(scaled, w_out, kinds, order=()):
    (rows, depth), hidden = scaled.shape, w_out.shape[0]
    return call(
        back_kernel,
        [shape((count, hidden), kind) for count, kind in kinds],
        (scaled, w_out),
        "back",
        order=order,
        flops=2 * rows * depth * hidden,
    )


def pass_kernel(to_high, to_low, low, high, plus, minus):
    def body(cols):
        plus[:, cols] = (to_high[:, cols] + low[:, cols].astype(F32)).astype(BF16)
        minus[:, cols] = (to_low[:, cols] + high[:, cols].astype(F32)).astype(BF16)

    each_block(plus.shape[1], body)


def sums_kernel(own, low, high, low_sum, high_sum, zero, to_high, plus, minus, to_low):
    def body(cols):
        upper = own[:128, cols] + high[:, cols].astype(F32) + low_sum[:, cols].astype(F32)
        lower = own[128:, cols] + low[:, cols].astype(F32) + high_sum[:, cols].astype(F32)
        zero[:, cols] = upper[:64]
        to_high[:, cols] = upper[64:96]
        plus[:, cols] = jnp.concatenate([upper[96:], lower[:32]], axis=0).astype(BF16)
        minus[:, cols] = lower[32:96].astype(BF16)
        to_low[:, cols] = lower[96:]

    each_block(own.shape[1], body)


def grad_kernel(own, low, high, low_sum, high_sum, slope, grad):
    def body(cols):
        upper = own[:32, cols] + high[32:, cols].astype(F32) + low_sum[:, cols].astype(F32)
        lower = own[32:, cols] + low[:32, cols].astype(F32) + high_sum[:, cols].astype(F32)
        back = jnp.concatenate([upper, lower], axis=0)
        grad[:, cols] = (back * slope[:, cols]).astype(BF16)

    each_block(own.shape[1], body)


def reduce_back(scaled, w_out, order_rest, order_sums):
    hidden = w_out.shape[0]
    half = [(128, BF16)] * 2
    plus, minus = back_rows(scaled[512:768], w_out, half)
    from_low, from_high = major(plus, 1), major(minus, -1)
    rest = jnp.concatenate([scaled[768:], scaled[:512]], axis=0)
    minus, to_low, own, to_high, plus = back_rows(
        rest, w_out, [(128, BF16), (128, F32), (256, F32), (128, F32), (128, BF16)], order_rest
    )
    low, high = major(plus, 1), major(minus, -1)
    plus, minus = call(pass_kernel, [shape((128, hidden), BF16)] * 2, (to_high, to_low, from_low, from_high), "pass")
    low_sum, high_sum = major(plus, 1), major(minus, -1)
    sums = call(
        sums_kernel,
        [shape((64, hidden), F32), shape((32, hidden), F32)]
        + [shape((64, hidden), BF16)] * 2
        + [shape((32, hidden), F32)],
        (own, low, high, low_sum, high_sum),
        "sums",
        order=order_sums,
    )

    def minor_parts(order):
        zero, to_high, plus, minus, to_low = sums
        low, high = minor(plus, 1), minor(minus, -1)
        plus, minus = call(
            pass_kernel,
            [shape((32, hidden), BF16)] * 2,
            (to_high, to_low, low[32:], high[:32]),
            "pass_minor",
            order=order,
        )
        return zero, low, high, minor(plus, 1), minor(minus, -1)

    return sums, minor_parts


def minor_sides(a):
    return minor(a, 1), minor(a, -1)


def minor_rows(a, low, high):
    return a, high, minor(low[:32], 1), minor(high[32:], -1), low


def stack_kernel(*refs):
    at = 0
    for piece in refs[:-1]:
        refs[-1][at : at + piece.shape[0], :] = piece[...]
        at += piece.shape[0]


def stack(pieces, order=()):
    dims = (sum(p.shape[0] for p in pieces), pieces[0].shape[1])
    return call(stack_kernel, [shape(dims, BF16)], pieces, "stack", order=order)[0]


def grad_inputs_kernel(*refs):
    *pieces, w, out = refs
    at = 0
    for piece in pieces:
        for k in range(0, piece.shape[0], 128):
            out[at : at + 128, :] = dot(piece[k : k + 128, :], w[...], NT)
            at += 128


def grad_inputs_rows(pieces, w_in, name, order=()):
    rows, depth, hidden = sum(p.shape[0] for p in pieces), *w_in.shape
    return call(
        grad_inputs_kernel,
        [shape((rows, depth), F32)],
        (*pieces, w_in),
        name,
        order=order,
        flops=2 * rows * depth * hidden,
    )[0]


def partial_rows(near, far, place, y, z):
    large, small = relative(place, y, z)
    spot = jnp.where(large == 3, 2, jnp.minimum(large, 1))
    return jnp.where(large == 2, far[rows_of(0, small), :], near[rows_of(spot, small), :])


def join_kernel(place, near, far, send, keep):
    for x in range(SIDE):
        for z in range(2):
            for out, core in ((keep, place[3]), (send, 1 - place[3])):
                block = partial_rows(near, far, place, place[2] + x, 2 * core + z)
                out[pl.ds(x * 128 + z * BLOCK, BLOCK), :] = block.astype(out.dtype)


def grad_w_in_kernel(factor, flipped, *refs):
    *pieces, out = refs

    def body(cols):
        rows = jnp.concatenate([piece[:, cols] for piece in pieces], axis=0)
        out[:, cols] = (dot(flipped[...], rows, NN) * factor).astype(BF16)

    each_block(out.shape[1], body, 2 * WIDE)


def grad_w_in_all(flipped, pieces, factor):
    hidden, depth = pieces[0].shape[1], flipped.shape[0]
    return call(
        functools.partial(grad_w_in_kernel, factor),
        [shape((depth, hidden), BF16)],
        (flipped, *pieces),
        "grad_w_in",
        flops=2 * 1024 * depth * hidden,
    )[0]


def flip_kernel(one, two, three, four, five, out):
    def body(cols):
        out[0, cols, :] = jnp.concatenate([one[:, cols], two[:, cols]], axis=0).T
        out[1, cols, :] = jnp.concatenate([three[:, cols], four[:, cols], five[:, cols]], axis=0).T

    each_block(one.shape[1], body)


def flip(rows, order):
    return call(flip_kernel, [shape((2, rows[0].shape[1], 128), BF16)], rows, "flip", order=order)[0]


def grad_w_out_kernel(factor, scaled, one, two, three, four, five, out):
    def body(cols):
        pieces = [p[k, cols, :] for p in (one, two, three, four, five) for k in range(p.shape[0])]
        out[cols, :] = (dot(jnp.concatenate(pieces, axis=1), scaled[...], NN) * factor).astype(BF16)

    each_block(out.shape[0], body, 2 * WIDE)


def grad_w_out_all(scaled, pieces, factor):
    depth, hidden = scaled.shape[1], pieces[0].shape[1]
    return call(
        functools.partial(grad_w_out_kernel, factor),
        [shape((hidden, depth), BF16)],
        (scaled, *pieces),
        "grad_w_out",
        flops=2 * 1024 * depth * hidden,
    )[0]


def row_gather(a):
    mine = stack((a, move_x(a, -1), move_x(a, -2), move_x(a, -3)))
    return mine, swap_core(mine)


def hold_kernel(a, out):
    out[...] = a[...]


def hold(a, order):
    return call(hold_kernel, [shape(a.shape, a.dtype)], (a,), "hold", order=order)[0]


def shards(inputs, upstream, preact, bias_in, w_in, w_out, lengths):
    col, row = lax.axis_index("col"), lax.axis_index("row")
    place = jnp.stack([col // SIDE, col % SIDE, row // 2, row % 2]).astype(jnp.int32)
    depth, hidden = w_in.shape
    factor = 1024 ** (-0.5)

    up_mine, up_other = row_gather(upstream)
    weight = call(weight_kernel, [shape((1024, 128), F32)], (lengths,), "weight", small=1)[0]
    pre = preact.astype(F32) + bias_in[None, :]
    value, slope = gelu_parts(pre)
    act, slope = lax.optimization_barrier((value.astype(BF16), slope))
    act_sides = minor_sides(act)
    scaled = call(
        scaled_kernel,
        [shape((1024, depth), BF16)],
        (place, up_mine, up_other, weight),
        "scaled",
        small=1,
        order=act_sides,
    )[0]
    act_rows = minor_rows(act, *act_sides)
    in_mine, in_other = row_gather(hold(inputs, (up_mine,)))
    in_flipped = call(
        inputs_kernel,
        [shape((depth, 1024), BF16)],
        (place, in_mine, in_other),
        "inputs",
        small=1,
        scratch=[pltpu.VMEM((1024, depth), BF16)],
    )[0]
    sums, minor_parts = reduce_back(scaled, w_out, (), act_rows)
    act_near = flip(act_rows, sums[:1])
    act_low, act_high = major(act_near, 1), major(act_near, -1)
    act_pieces = (act_near, act_high, major(act_low[:1], 1), major(act_high[1:], -1), act_low)

    parts = minor_parts((act_near,))
    grad = call(grad_kernel, [shape((BLOCK, hidden), BF16)], (*parts, slope), "grad_pre", order=(act_low, act_high))[0]
    grad_w_out = grad_w_out_all(scaled, act_pieces, factor)
    near = stack(minor_rows(grad, *minor_sides(grad)), (*act_pieces[2:4], in_flipped))
    low_a, high_b = major(near[:128], 1), major(near[128:], -1)
    low_b, high_a = major(near[128:], 1), major(near[:128], -1)
    far = major(low_a, 1), major(high_b, -1)
    total_near = grad_inputs_rows((near, high_a, high_b, low_a, low_b), w_in, "grad_inputs_near")
    total_far = grad_inputs_rows(far, w_in, "grad_inputs_far", (total_near, grad_w_out))
    pieces = (near, high_a, high_b, *far, low_a, low_b)
    send, keep = call(
        join_kernel,
        [shape((512, depth), BF16), shape((512, depth), F32)],
        (place, total_near, total_far),
        "join",
        small=1,
    )
    keep = keep + swap_core(send).astype(F32)
    parts = [keep[128 * k : 128 * (k + 1)] for k in range(SIDE)]
    grad_inputs = parts[0]
    for k in range(1, SIDE):
        grad_inputs = grad_inputs + move_x(parts[k].astype(BF16), k).astype(F32)
    grad_w_in = grad_w_in_all(in_flipped, pieces, factor)
    return (grad_inputs.astype(BF16), grad_w_in, grad_w_out)


def solution(mesh):
    placed = (
        P("row", "col"),
        P("row", "col"),
        P("col", "row"),
        P("row"),
        P("col", "row"),
        P("row", "col"),
        P(),
    )
    return jax.shard_map(
        shards,
        mesh=mesh,
        in_specs=placed,
        out_specs=(P("row", "col"), P("col", "row"), P("row", "col")),
        check_vma=False,
    )
```
